32 devices in a mesh: wide: 8 (over y, x, core), narrow: 4 (over z).
Axes of the slice: x: 2, y: 2, z: 4, core: 2. Of those that a mesh axis runs over, the one named last changes fastest.
Arguments:
- velocity: bfloat16 [3, 12288, 12288], P(None, 'narrow', 'wide'), may hold values from -6 to 6
Outputs:
- dudx: bfloat16 [3, 12288, 12288], P(None, 'narrow', 'wide')
- dudy: bfloat16 [3, 12288, 12288], P(None, 'narrow', 'wide')
The draws below stay inside these ranges and needn't reach their ends.
All inputs are finite; a program needn't handle non-finite values.
Results may differ from the reference program's by a relative error of at most 0.001.
Values may be sent and summed in bfloat16 or wider, within the bound.
A program may use at most 576 MiB of HBM per device.

```python
import jax
import jax.numpy as jnp
from jax import lax

NX = 12288
NY = 12288
NZ = 3


def steps_of(stream_key, extent, pieces, smallest, top_value):
    def one(axis_at, shards_of):
        heights = jax.random.uniform(jax.random.fold_in(jax.random.fold_in(stream_key, 6), axis_at), (shards_of,), jnp.float32, smallest / len(pieces), top_value / len(pieces))
        return jnp.repeat(jnp.exp(heights), extent[axis_at] // shards_of).reshape((-1,) + (1,) * (len(extent) - axis_at - 1))

    gain = one(*pieces[0])
    for cut in pieces[1:]:
        gain = gain * one(*cut)
    return gain


def noise(key, shape, width, bound, cuts=(), held_as=jnp.bfloat16):
    loudness = steps_of(key, shape, cuts, -0.22, 0.18) if cuts else 1.0
    array = jax.random.normal(key, shape, jnp.float32) * width * loudness
    return jnp.minimum(jnp.maximum(array, -bound), bound).astype(held_as)


def setup_inputs(seed: int = 0) -> dict:
    streams_of = jax.random.split(jax.random.key(seed), 2)
    velocity = noise(streams_of[0], (NZ, NX, NY), 1.0, 6.0, ((1, 4), (2, 8)))
    return {"velocity": velocity}


def right_side(field, along):
    plus_one = jnp.roll(field, -1, along)
    minus_one = jnp.roll(field, 1, along)
    plus_two = jnp.roll(field, -2, along)
    minus_two = jnp.roll(field, 2, along)
    return (7.0 / 9.0) * (plus_one - minus_one) + (1.0 / 36.0) * (plus_two - minus_two)


def cyclic_solve(source, along):
    length = source.shape[along]
    wavenum = jnp.arange(length // 2 + 1).astype(source.dtype)
    divisor = 1.0 + (2.0 / 3.0) * jnp.cos(2.0 * jnp.pi * wavenum / length)
    if along == 0:
        divisor = divisor[:, None]
    spectrum = jnp.fft.rfft(source, axis=along) / divisor
    return jnp.fft.irfft(spectrum, n=length, axis=along)


def one_plane(plane):
    field = plane.astype(jnp.float32)
    deriv_x = cyclic_solve(right_side(field, 0), 0).astype(jnp.bfloat16)
    deriv_y = cyclic_solve(right_side(field, 1), 1).astype(jnp.bfloat16)
    return deriv_x, deriv_y


def reference(velocity):
    dudx, dudy = lax.map(one_plane, velocity)
    return dudx, dudy
```

```python
import math

import jax
import jax.numpy as jnp
import numpy as np
from jax import lax
from jax.experimental import pallas as pl
from jax.experimental.pallas import tpu as pltpu
from jax.sharding import PartitionSpec as P

RATIO = (math.sqrt(5.0) - 3.0) / 2.0
FACTOR = 3.0 / math.sqrt(5.0)
COEF_NEAR = 7.0 / 9.0
COEF_FAR = 1.0 / 36.0
HALO = 32
SCALE = 1.596
NUDGE = 2.0**-15
WINDOW = 256
OUT_ROWS = WINDOW - 2 * HALO
LANES = 128


def solve_weight(offset):
    return FACTOR * np.power(RATIO, np.abs(offset))


def weight_table(outputs, inputs):
    offset = np.asarray(inputs)[None, :] - np.asarray(outputs)[:, None]
    coeff = COEF_NEAR * (solve_weight(offset - 1) - solve_weight(offset + 1))
    coeff = coeff + COEF_FAR * (solve_weight(offset - 2) - solve_weight(offset + 2))
    coeff = coeff / SCALE + np.where(np.abs(offset) == 6, np.sign(offset) * NUDGE, 0.0)
    return jnp.asarray(coeff.astype(np.float32)).astype(jnp.bfloat16)


def mix(a, b):
    return lax.dot_general(a, b, (((1,), (0,)), ((), ())), preferred_element_type=jnp.float32)


def main_kernel(x_ref, prev_ref, next_ref, tx_ref, ty_ref, dx_ref, dy_ref):
    rows, cols = x_ref.shape
    for top in range(0, rows, OUT_ROWS):
        low, high = top - HALO, top - HALO + WINDOW
        parts = []
        if low < 0:
            parts.append(prev_ref[...])
        parts.append(x_ref[max(low, 0) : min(high, rows), :])
        if high > rows:
            parts.append(next_ref[...])
        window = jnp.concatenate(parts, axis=0) if len(parts) > 1 else parts[0]
        result = mix(tx_ref[...], window) * SCALE
        dx_ref[top : top + OUT_ROWS, :] = result.astype(dx_ref.dtype)
    for left in range(0, cols, 2 * LANES):
        right = min(left + 2 * LANES, cols)
        low, high = max(left - LANES, 0), min(right + LANES, cols)
        start = low - (left - LANES)
        table = ty_ref[start : start + high - low, : right - left]
        result = mix(x_ref[:, low:high], table) * SCALE
        dy_ref[:, left:right] = result.astype(dy_ref.dtype)


def edge_kernel(
    dx_in, dy_in, halo_y_ref, cur_ref, inner_ref, halo_x_ref, near_ref, far_ref,
    ty_halo_ref, ty_cur_ref, ty_in_ref, tx_halo_ref, tx_near_ref, tx_far_ref, dx_ref, dy_ref,
):
    result = lax.dot_general(
        halo_y_ref[...], ty_halo_ref[...], (((0,), (0,)), ((), ())), preferred_element_type=jnp.float32
    )
    result = result + mix(cur_ref[...], ty_cur_ref[...]) + mix(inner_ref[...], ty_in_ref[...])
    dy_ref[...] = (result * SCALE).astype(dy_ref.dtype)
    result = mix(tx_halo_ref[...], halo_x_ref[...])
    result = result + mix(tx_near_ref[...], near_ref[...]) + mix(tx_far_ref[...], far_ref[...])
    dx_ref[...] = (result * SCALE).astype(dx_ref.dtype)


def halos(ends, axis):
    devices = lax.axis_size(axis)
    up = [(i, (i + 1) % devices) for i in range(devices)]
    down = [(j, i) for i, j in up]
    leading, last = ends
    return jnp.stack([lax.ppermute(last, axis, up), lax.ppermute(leading, axis, down)])


def pick_rows(rows, limit):
    best = OUT_ROWS
    for n in range(OUT_ROWS, limit + 1, OUT_ROWS):
        if rows % n == 0:
            best = n
    return best


def shards(velocity):
    planes, rows, cols = velocity.shape
    ends_y = (
        jnp.transpose(velocity[:, :, :HALO], (0, 2, 1)),
        jnp.transpose(velocity[:, :, cols - HALO :], (0, 2, 1)),
    )
    halo_y = halos(ends_y, "wide")
    halo_x = halos((velocity[:, :HALO], velocity[:, rows - HALO :]), "narrow")

    tile = pick_rows(rows, 384)
    per = tile // HALO
    strips = rows // HALO
    tx = weight_table(np.arange(OUT_ROWS) + HALO, np.arange(WINDOW))
    ty = weight_table(np.arange(2 * LANES) + LANES, np.arange(4 * LANES)).T
    shape = jax.ShapeDtypeStruct(velocity.shape, velocity.dtype)
    full = pl.BlockSpec((None, tile, cols), lambda z, i: (z, i, 0))
    size = planes * rows * cols
    dx, dy = pl.pallas_call(
        main_kernel,
        grid=(planes, rows // tile),
        in_specs=[
            full,
            pl.BlockSpec((None, HALO, cols), lambda z, i: (z, jnp.maximum(i * per - 1, 0), 0)),
            pl.BlockSpec((None, HALO, cols), lambda z, i: (z, jnp.minimum((i + 1) * per, strips - 1), 0)),
            pl.BlockSpec(tx.shape, lambda z, i: (0, 0)),
            pl.BlockSpec(ty.shape, lambda z, i: (0, 0)),
        ],
        out_specs=[full, full],
        out_shape=[shape, shape],
        cost_estimate=pl.CostEstimate(flops=size * 2 * 1024, bytes_accessed=size * 6, transcendentals=0),
        compiler_params=pltpu.CompilerParams(vmem_limit_bytes=48 * 2**20),
    )(velocity, velocity, velocity, tx, ty)

    here = np.arange(LANES)
    before, after = (np.arange(-HALO, 0), np.arange(LANES, LANES + HALO))
    ty_halo = jnp.stack([weight_table(here, before).T, weight_table(here, after).T])
    ty_cur = weight_table(here, here).T
    ty_in = jnp.stack([weight_table(here, here + LANES).T, weight_table(here, here - LANES).T])
    edge = np.arange(HALO)
    tx_halo = jnp.stack([weight_table(edge, edge - HALO), weight_table(edge, edge + HALO)])
    tx_near = weight_table(edge, edge)
    tx_far = jnp.stack([weight_table(edge, edge + HALO), weight_table(edge, edge - HALO)])
    blocks = cols // LANES

    def whole(table):
        return pl.BlockSpec(table.shape, lambda s, z: (0, 0))

    def sided(table):
        return pl.BlockSpec((None,) + table.shape[1:], lambda s, z: (s, 0, 0))

    lanes_out = pl.BlockSpec((None, rows, LANES), lambda s, z: (z, 0, s * (blocks - 1)))
    rows_out = pl.BlockSpec((None, HALO, cols), lambda s, z: (z, s * (strips - 1), 0))
    any_spec = pl.BlockSpec(memory_space=pl.ANY)
    return pl.pallas_call(
        edge_kernel,
        grid=(2, planes),
        in_specs=[
            any_spec,
            any_spec,
            pl.BlockSpec((None, None, HALO, rows), lambda s, z: (s, z, 0, 0)),
            lanes_out,
            pl.BlockSpec((None, rows, LANES), lambda s, z: (z, 0, s * (blocks - 3) + 1)),
            pl.BlockSpec((None, None, HALO, cols), lambda s, z: (s, z, 0, 0)),
            rows_out,
            pl.BlockSpec((None, HALO, cols), lambda s, z: (z, s * (strips - 3) + 1, 0)),
            sided(ty_halo), whole(ty_cur), sided(ty_in), sided(tx_halo), whole(tx_near), sided(tx_far),
        ],
        out_specs=[rows_out, lanes_out],
        out_shape=[shape, shape],
        input_output_aliases={0: 0, 1: 1},
        cost_estimate=pl.CostEstimate(flops=size * 64, bytes_accessed=size, transcendentals=0),
        compiler_params=pltpu.CompilerParams(vmem_limit_bytes=48 * 2**20),
    )(dx, dy, halo_y, velocity, velocity, halo_x, velocity, velocity,
      ty_halo, ty_cur, ty_in, tx_halo, tx_near, tx_far)


def solution(mesh):
    placed = P(None, "narrow", "wide")
    return jax.shard_map(
        shards, mesh=mesh, in_specs=(placed,), out_specs=(placed, placed), check_vma=False
    )
```

```python
import math

import jax
import jax.numpy as jnp
import numpy as np
from jax import lax
from jax.experimental import pallas as pl
from jax.experimental.pallas import tpu as pltpu
from jax.sharding import PartitionSpec as P

RATIO = (math.sqrt(5.0) - 3.0) / 2.0
FACTOR = 3.0 / math.sqrt(5.0)
COEF_NEAR = 7.0 / 9.0
COEF_FAR = 1.0 / 36.0
HALO = 32
SCALE = 1.596
NUDGE = 2.0**-15
WINDOW = 256
PACK = 16
OUT_ROWS = WINDOW - 2 * HALO
LANES = 128


def solve_weight(offset):
    return FACTOR * np.power(RATIO, np.abs(offset))


def weight_table(outputs, inputs):
    offset = np.asarray(inputs)[None, :] - np.asarray(outputs)[:, None]
    coeff = COEF_NEAR * (solve_weight(offset - 1) - solve_weight(offset + 1))
    coeff = coeff + COEF_FAR * (solve_weight(offset - 2) - solve_weight(offset + 2))
    coeff = coeff / SCALE + np.where(np.abs(offset) == 6, np.sign(offset) * NUDGE, 0.0)
    return jnp.asarray(coeff.astype(np.float32)).astype(jnp.bfloat16)


def mix(a, b):
    return lax.dot_general(a, b, (((1,), (0,)), ((), ())), preferred_element_type=jnp.float32)


def pack_tables():
    cell = np.arange(LANES)
    lead, last = (np.zeros((PACK, LANES)), np.zeros((PACK, LANES)))
    for i in range(PACK - 1):
        lead[i, i] = 1.0
        last[PACK - 1 - i, LANES - 1 - i] = 1.0
    tail = np.where(cell >= PACK - 1, np.power(RATIO, np.maximum(cell - PACK + 1, 0)), 0.0)
    lead[PACK - 1], last[0] = (tail, tail[::-1])
    return jnp.asarray(np.stack([last, lead]).astype(np.float32)).astype(jnp.bfloat16)


def exchange_kernel(
    x_ref, table_ref, halo_y_ref, halo_x_ref,
    edge_y, edge_x, out_y, out_x, load_sem, send_sem, recv_sem,
):
    planes, rows, cols = x_ref.shape
    depth = edge_x.shape[2]
    loads = []
    for z in range(planes):
        for side in range(2):
            col = (cols - LANES) if side == 0 else 0
            row = (rows - depth) if side == 0 else 0
            loads.append(pltpu.make_async_copy(
                x_ref.at[z, :, pl.ds(col, LANES)], edge_y.at[side, z], load_sem.at[0, side, z]))
            loads.append(pltpu.make_async_copy(
                x_ref.at[z, pl.ds(row, depth), :], edge_x.at[side, z], load_sem.at[1, side, z]))
    for load in loads:
        load.start()

    targets = []
    for axis in ("wide", "narrow"):
        size = lax.axis_size(axis)
        me = lax.axis_index(axis)
        targets.append(({axis: lax.rem(me + 1, size)}, {axis: lax.rem(me + size - 1, size)}))
    barrier = pltpu.get_barrier_semaphore()
    for pair in targets:
        for target in pair:
            pl.semaphore_signal(barrier, inc=1, device_id=target, device_id_type=pl.DeviceIdType.MESH)
    pl.semaphore_wait(barrier, 4)

    sends = []
    at = 0
    for z in range(planes):
        for side in range(2):
            loads[at].wait()
            packed = lax.dot_general(
                table_ref[side], edge_y[side, z], (((1,), (1,)), ((), ())),
                preferred_element_type=jnp.float32)
            out_y[side, z] = packed.astype(out_y.dtype)
            sends.append(pltpu.make_async_remote_copy(
                out_y.at[side, z], halo_y_ref.at[side, z], send_sem.at[0, side, z],
                recv_sem.at[0, side, z], device_id=targets[0][side],
                device_id_type=pl.DeviceIdType.MESH))
            sends[-1].start()
            loads[at + 1].wait()
            cut = (LANES - depth) if side == 0 else 0
            packed = mix(table_ref[side][:, cut : cut + depth], edge_x[side, z])
            out_x[side, z] = packed.astype(out_x.dtype)
            sends.append(pltpu.make_async_remote_copy(
                out_x.at[side, z], halo_x_ref.at[side, z], send_sem.at[1, side, z],
                recv_sem.at[1, side, z], device_id=targets[1][side],
                device_id_type=pl.DeviceIdType.MESH))
            sends[-1].start()
            at += 2
    for send in sends:
        send.wait()


def exchange(velocity):
    planes, rows, cols = velocity.shape
    depth = LANES
    dtype = velocity.dtype
    shape_y, shape_x = ((2, planes, PACK, rows), (2, planes, PACK, cols))
    return pl.pallas_call(
        exchange_kernel,
        in_specs=[pl.BlockSpec(memory_space=pl.ANY), pl.BlockSpec(memory_space=pltpu.VMEM)],
        out_specs=[pl.BlockSpec(memory_space=pl.ANY)] * 2,
        out_shape=[jax.ShapeDtypeStruct(shape_y, dtype), jax.ShapeDtypeStruct(shape_x, dtype)],
        scratch_shapes=[
            pltpu.VMEM((2, planes, rows, LANES), dtype),
            pltpu.VMEM((2, planes, depth, cols), dtype),
            pltpu.VMEM(shape_y, dtype),
            pltpu.VMEM(shape_x, dtype),
            pltpu.SemaphoreType.DMA((2, 2, planes)),
            pltpu.SemaphoreType.DMA((2, 2, planes)),
            pltpu.SemaphoreType.DMA((2, 2, planes)),
        ],
        compiler_params=pltpu.CompilerParams(
            collective_id=0, has_side_effects=True, vmem_limit_bytes=48 * 2**20),
    )(velocity, pack_tables())


def main_kernel(
    x_ref, prev_ref, next_ref, before_x_ref, after_x_ref, before_y_ref, after_y_ref,
    tx_ref, ty_ref, th_ref, dx_ref, dy_ref,
):
    rows, cols = x_ref.shape
    step, steps = (pl.program_id(1), pl.num_programs(1))
    empty = jnp.zeros((HALO - PACK, cols), x_ref.dtype)
    for top in range(0, rows, OUT_ROWS):
        low, high = top - HALO, top - HALO + WINDOW
        parts = []
        if low < 0:
            outside = jnp.concatenate([empty, before_x_ref[...]], axis=0)
            parts.append(jnp.where(step == 0, outside, prev_ref[...]))
        parts.append(x_ref[max(low, 0) : min(high, rows), :])
        if high > rows:
            outside = jnp.concatenate([after_x_ref[...], empty], axis=0)
            parts.append(jnp.where(step == steps - 1, outside, next_ref[...]))
        window = jnp.concatenate(parts, axis=0) if len(parts) > 1 else parts[0]
        result = mix(tx_ref[...], window) * SCALE
        dx_ref[top : top + OUT_ROWS, :] = result.astype(dx_ref.dtype)
    for left in range(0, cols, 2 * LANES):
        right = min(left + 2 * LANES, cols)
        low, high = max(left - LANES, 0), min(right + LANES, cols)
        start = low - (left - LANES)
        table = ty_ref[start : start + high - low, : right - left]
        result = mix(x_ref[:, low:high], table)
        blocks = [result[:, k : k + LANES] for k in range(0, right - left, LANES)]
        if left == 0:
            blocks[0] = blocks[0] + mix_first(before_y_ref[...], th_ref[0])
        if right == cols:
            blocks[-1] = blocks[-1] + mix_first(after_y_ref[...], th_ref[1])
        for k, block in enumerate(blocks):
            dy_ref[:, left + k * LANES : left + (k + 1) * LANES] = (block * SCALE).astype(dy_ref.dtype)


def mix_first(a, b):
    return lax.dot_general(a, b, (((0,), (0,)), ((), ())), preferred_element_type=jnp.float32)


def pick_rows(rows, limit):
    best = OUT_ROWS
    for n in range(OUT_ROWS, limit + 1, OUT_ROWS):
        if rows % n == 0:
            best = n
    return best


def shards(velocity):
    planes, rows, cols = velocity.shape
    halo_y, halo_x = exchange(velocity)
    tile = pick_rows(rows, 768)
    per = tile // HALO
    strips = rows // HALO
    tx = weight_table(np.arange(OUT_ROWS) + HALO, np.arange(WINDOW))
    ty = weight_table(np.arange(2 * LANES) + LANES, np.arange(4 * LANES)).T
    here = np.arange(LANES)
    th = jnp.stack([
        weight_table(here, np.arange(-PACK, 0)).T,
        weight_table(here, np.arange(LANES, LANES + PACK)).T,
    ])
    shape = jax.ShapeDtypeStruct(velocity.shape, velocity.dtype)
    full = pl.BlockSpec((None, tile, cols), lambda z, i: (z, i, 0))
    size = planes * rows * cols

    def ends_x(side):
        return pl.BlockSpec((None, None, PACK, cols), lambda z, i: (side, z, 0, 0))

    def ends_y(side):
        return pl.BlockSpec((None, None, PACK, tile), lambda z, i: (side, z, 0, i))

    return pl.pallas_call(
        main_kernel,
        grid=(planes, rows // tile),
        in_specs=[
            full,
            pl.BlockSpec((None, HALO, cols), lambda z, i: (z, jnp.maximum(i * per - 1, 0), 0)),
            pl.BlockSpec((None, HALO, cols), lambda z, i: (z, jnp.minimum((i + 1) * per, strips - 1), 0)),
            ends_x(0), ends_x(1), ends_y(0), ends_y(1),
            pl.BlockSpec(tx.shape, lambda z, i: (0, 0)),
            pl.BlockSpec(ty.shape, lambda z, i: (0, 0)),
            pl.BlockSpec(th.shape, lambda z, i: (0, 0, 0)),
        ],
        out_specs=[full, full],
        out_shape=[shape, shape],
        cost_estimate=pl.CostEstimate(flops=size * 2 * 1024, bytes_accessed=size * 6, transcendentals=0),
        compiler_params=pltpu.CompilerParams(vmem_limit_bytes=48 * 2**20),
    )(velocity, velocity, velocity, halo_x, halo_x, halo_y, halo_y, tx, ty, th)


def solution(mesh):
    placed = P(None, "narrow", "wide")
    return jax.shard_map(
        shards, mesh=mesh, in_specs=(placed,), out_specs=(placed, placed), check_vma=False
    )
```

```python
import math

import jax
import jax.numpy as jnp
import numpy as np
from jax import lax
from jax.experimental import pallas as pl
from jax.experimental.pallas import tpu as pltpu
from jax.sharding import PartitionSpec as P

RATIO = (math.sqrt(5.0) - 3.0) / 2.0
FACTOR = 3.0 / math.sqrt(5.0)
COEF_NEAR = 7.0 / 9.0
COEF_FAR = 1.0 / 36.0
HALO = 32
SCALE = 1.596
NUDGE = 2.0**-15
WINDOW = 256
PACK = 16
OUT_ROWS = WINDOW - 2 * HALO
LANES = 128


def solve_weight(offset):
    return FACTOR * np.power(RATIO, np.abs(offset))


def weight_table(outputs, inputs):
    offset = np.asarray(inputs)[None, :] - np.asarray(outputs)[:, None]
    coeff = COEF_NEAR * (solve_weight(offset - 1) - solve_weight(offset + 1))
    coeff = coeff + COEF_FAR * (solve_weight(offset - 2) - solve_weight(offset + 2))
    coeff = coeff / SCALE + np.where(np.abs(offset) == 6, np.sign(offset) * NUDGE, 0.0)
    return jnp.asarray(coeff.astype(np.float32)).astype(jnp.bfloat16)


def mix(a, b):
    return lax.dot_general(a, b, (((1,), (0,)), ((), ())), preferred_element_type=jnp.float32)


def pack_tables():
    cell = np.arange(LANES)
    lead, last = (np.zeros((PACK, LANES)), np.zeros((PACK, LANES)))
    for i in range(PACK - 1):
        lead[i, i] = 1.0
        last[PACK - 1 - i, LANES - 1 - i] = 1.0
    tail = np.where(cell >= PACK - 1, np.power(RATIO, np.maximum(cell - PACK + 1, 0)), 0.0)
    lead[PACK - 1], last[0] = (tail, tail[::-1])
    return jnp.asarray(np.stack([last, lead]).astype(np.float32)).astype(jnp.bfloat16)


def exchange_kernel(
    x_ref, table_ref, halo_y_ref, halo_x_ref,
    edge_y, edge_x, out_y, out_x, load_sem, send_sem, recv_sem,
):
    planes, rows, cols = x_ref.shape
    depth = edge_x.shape[2]
    loads = []
    for z in range(planes):
        for side in range(2):
            col = (cols - LANES) if side == 0 else 0
            row = (rows - depth) if side == 0 else 0
            loads.append(pltpu.make_async_copy(
                x_ref.at[z, :, pl.ds(col, LANES)], edge_y.at[side, z], load_sem.at[0, side, z]))
            loads.append(pltpu.make_async_copy(
                x_ref.at[z, pl.ds(row, depth), :], edge_x.at[side, z], load_sem.at[1, side, z]))
    targets = []
    for axis in ("wide", "narrow"):
        size = lax.axis_size(axis)
        me = lax.axis_index(axis)
        targets.append(({axis: lax.rem(me + 1, size)}, {axis: lax.rem(me + size - 1, size)}))
    barrier = pltpu.get_barrier_semaphore()
    for pair in targets:
        for target in pair:
            pl.semaphore_signal(barrier, inc=1, device_id=target, device_id_type=pl.DeviceIdType.MESH)

    for load in loads:
        load.start()
    sends = []
    at = 0
    for z in range(planes):
        for side in range(2):
            loads[at].wait()
            packed = lax.dot_general(
                table_ref[side], edge_y[side, z], (((1,), (1,)), ((), ())),
                preferred_element_type=jnp.float32)
            out_y[side, z] = packed.astype(out_y.dtype)
            if not sends:
                pl.semaphore_wait(barrier, 4)
            sends.append(pltpu.make_async_remote_copy(
                out_y.at[side, z], halo_y_ref.at[side, z], send_sem.at[0, side, z],
                recv_sem.at[0, side, z], device_id=targets[0][side],
                device_id_type=pl.DeviceIdType.MESH))
            sends[-1].start()
            loads[at + 1].wait()
            cut = (LANES - depth) if side == 0 else 0
            packed = mix(table_ref[side][:, cut : cut + depth], edge_x[side, z])
            out_x[side, z] = packed.astype(out_x.dtype)
            sends.append(pltpu.make_async_remote_copy(
                out_x.at[side, z], halo_x_ref.at[side, z], send_sem.at[1, side, z],
                recv_sem.at[1, side, z], device_id=targets[1][side],
                device_id_type=pl.DeviceIdType.MESH))
            sends[-1].start()
            at += 2
    for send in sends:
        send.wait()


def exchange(velocity):
    planes, rows, cols = velocity.shape
    depth = LANES // 2
    dtype = velocity.dtype
    shape_y, shape_x = ((2, planes, PACK, rows), (2, planes, PACK, cols))
    return pl.pallas_call(
        exchange_kernel,
        in_specs=[pl.BlockSpec(memory_space=pl.ANY), pl.BlockSpec(memory_space=pltpu.VMEM)],
        out_specs=[pl.BlockSpec(memory_space=pl.ANY)] * 2,
        out_shape=[jax.ShapeDtypeStruct(shape_y, dtype), jax.ShapeDtypeStruct(shape_x, dtype)],
        scratch_shapes=[
            pltpu.VMEM((2, planes, rows, LANES), dtype),
            pltpu.VMEM((2, planes, depth, cols), dtype),
            pltpu.VMEM(shape_y, dtype),
            pltpu.VMEM(shape_x, dtype),
            pltpu.SemaphoreType.DMA((2, 2, planes)),
            pltpu.SemaphoreType.DMA((2, 2, planes)),
            pltpu.SemaphoreType.DMA((2, 2, planes)),
        ],
        compiler_params=pltpu.CompilerParams(
            collective_id=0, has_side_effects=True, vmem_limit_bytes=48 * 2**20),
    )(velocity, pack_tables())


def main_kernel(
    x_ref, prev_ref, next_ref, before_x_ref, after_x_ref, before_y_ref, after_y_ref,
    tx_ref, ty_ref, th_ref, dx_ref, dy_ref,
):
    rows, cols = x_ref.shape
    step, steps = (pl.program_id(1), pl.num_programs(1))
    empty = jnp.zeros((HALO - PACK, cols), x_ref.dtype)
    for top in range(0, rows, OUT_ROWS):
        low, high = top - HALO, top - HALO + WINDOW
        parts = []
        if low < 0:
            outside = jnp.concatenate([empty, before_x_ref[...]], axis=0)
            parts.append(jnp.where(step == 0, outside, prev_ref[...]))
        parts.append(x_ref[max(low, 0) : min(high, rows), :])
        if high > rows:
            outside = jnp.concatenate([after_x_ref[...], empty], axis=0)
            parts.append(jnp.where(step == steps - 1, outside, next_ref[...]))
        window = jnp.concatenate(parts, axis=0) if len(parts) > 1 else parts[0]
        result = mix(tx_ref[...], window) * SCALE
        dx_ref[top : top + OUT_ROWS, :] = result.astype(dx_ref.dtype)
    for left in range(0, cols, 2 * LANES):
        right = min(left + 2 * LANES, cols)
        low, high = max(left - LANES, 0), min(right + LANES, cols)
        start = low - (left - LANES)
        table = ty_ref[start : start + high - low, : right - left]
        result = mix(x_ref[:, low:high], table)
        blocks = [result[:, k : k + LANES] for k in range(0, right - left, LANES)]
        if left == 0:
            blocks[0] = blocks[0] + mix_first(before_y_ref[...], th_ref[0])
        if right == cols:
            blocks[-1] = blocks[-1] + mix_first(after_y_ref[...], th_ref[1])
        for k, block in enumerate(blocks):
            dy_ref[:, left + k * LANES : left + (k + 1) * LANES] = (block * SCALE).astype(dy_ref.dtype)


def mix_first(a, b):
    return lax.dot_general(a, b, (((0,), (0,)), ((), ())), preferred_element_type=jnp.float32)


def pick_rows(rows, limit):
    best = OUT_ROWS
    for n in range(OUT_ROWS, limit + 1, OUT_ROWS):
        if rows % n == 0:
            best = n
    return best


def shards(velocity):
    planes, rows, cols = velocity.shape
    halo_y, halo_x = exchange(velocity)
    tile = pick_rows(rows, 768)
    per = tile // HALO
    strips = rows // HALO
    tx = weight_table(np.arange(OUT_ROWS) + HALO, np.arange(WINDOW))
    ty = weight_table(np.arange(2 * LANES) + LANES, np.arange(4 * LANES)).T
    here = np.arange(LANES)
    th = jnp.stack([
        weight_table(here, np.arange(-PACK, 0)).T,
        weight_table(here, np.arange(LANES, LANES + PACK)).T,
    ])
    shape = jax.ShapeDtypeStruct(velocity.shape, velocity.dtype)
    full = pl.BlockSpec((None, tile, cols), lambda z, i: (z, i, 0))
    size = planes * rows * cols

    def ends_x(side):
        return pl.BlockSpec((None, None, PACK, cols), lambda z, i: (side, z, 0, 0))

    def ends_y(side):
        return pl.BlockSpec((None, None, PACK, tile), lambda z, i: (side, z, 0, i))

    return pl.pallas_call(
        main_kernel,
        grid=(planes, rows // tile),
        in_specs=[
            full,
            pl.BlockSpec((None, HALO, cols), lambda z, i: (z, jnp.maximum(i * per - 1, 0), 0)),
            pl.BlockSpec((None, HALO, cols), lambda z, i: (z, jnp.minimum((i + 1) * per, strips - 1), 0)),
            ends_x(0), ends_x(1), ends_y(0), ends_y(1),
            pl.BlockSpec(tx.shape, lambda z, i: (0, 0)),
            pl.BlockSpec(ty.shape, lambda z, i: (0, 0)),
            pl.BlockSpec(th.shape, lambda z, i: (0, 0, 0)),
        ],
        out_specs=[full, full],
        out_shape=[shape, shape],
        cost_estimate=pl.CostEstimate(flops=size * 2 * 1024, bytes_accessed=size * 6, transcendentals=0),
        compiler_params=pltpu.CompilerParams(vmem_limit_bytes=48 * 2**20),
    )(velocity, velocity, velocity, halo_x, halo_x, halo_y, halo_y, tx, ty, th)


def solution(mesh):
    placed = P(None, "narrow", "wide")
    return jax.shard_map(
        shards, mesh=mesh, in_specs=(placed,), out_specs=(placed, placed), check_vma=False
    )
```

```python
import math

import jax
import jax.numpy as jnp
import numpy as np
from jax import lax
from jax.experimental import pallas as pl
from jax.experimental.pallas import tpu as pltpu
from jax.sharding import PartitionSpec as P

RATIO = (math.sqrt(5.0) - 3.0) / 2.0
FACTOR = 3.0 / math.sqrt(5.0)
COEF_NEAR = 7.0 / 9.0
COEF_FAR = 1.0 / 36.0
HALO = 32
SCALE = 1.596
NUDGE = 2.0**-15
WINDOW = 256
PACK = 16
OUT_ROWS = WINDOW - 2 * HALO
LANES = 128


def solve_weight(offset):
    return FACTOR * np.power(RATIO, np.abs(offset))


def weight_table(outputs, inputs):
    offset = np.asarray(inputs)[None, :] - np.asarray(outputs)[:, None]
    coeff = COEF_NEAR * (solve_weight(offset - 1) - solve_weight(offset + 1))
    coeff = coeff + COEF_FAR * (solve_weight(offset - 2) - solve_weight(offset + 2))
    coeff = coeff / SCALE + np.where(np.abs(offset) == 6, np.sign(offset) * NUDGE, 0.0)
    return jnp.asarray(coeff.astype(np.float32)).astype(jnp.bfloat16)


def mix(a, b):
    return lax.dot_general(a, b, (((1,), (0,)), ((), ())), preferred_element_type=jnp.float32)


def pack_tables():
    cell = np.arange(LANES)
    lead, last = (np.zeros((PACK, LANES)), np.zeros((PACK, LANES)))
    for i in range(PACK - 1):
        lead[i, i] = 1.0
        last[PACK - 1 - i, LANES - 1 - i] = 1.0
    tail = np.where(cell >= PACK - 1, np.power(RATIO, np.maximum(cell - PACK + 1, 0)), 0.0)
    lead[PACK - 1], last[0] = (tail, tail[::-1])
    return jnp.asarray(np.stack([last, lead]).astype(np.float32)).astype(jnp.bfloat16)


def exchange_kernel(
    x_ref, table_ref, halo_y_ref, halo_x_ref,
    edge_y, edge_x, out_y, out_x, load_sem, send_sem, recv_sem,
):
    planes, rows, cols = x_ref.shape
    depth = edge_x.shape[2]
    loads = []
    for z in range(planes):
        for side in range(2):
            col = (cols - LANES) if side == 0 else 0
            row = (rows - depth) if side == 0 else 0
            loads.append(pltpu.make_async_copy(
                x_ref.at[z, :, pl.ds(col, LANES)], edge_y.at[side, z], load_sem.at[0, side, z]))
            loads.append(pltpu.make_async_copy(
                x_ref.at[z, pl.ds(row, depth), :], edge_x.at[side, z], load_sem.at[1, side, z]))
    targets = []
    for axis in ("wide", "narrow"):
        size = lax.axis_size(axis)
        me = lax.axis_index(axis)
        targets.append(({axis: lax.rem(me + 1, size)}, {axis: lax.rem(me + size - 1, size)}))
    barrier = pltpu.get_barrier_semaphore()
    for pair in targets:
        for target in pair:
            pl.semaphore_signal(barrier, inc=1, device_id=target, device_id_type=pl.DeviceIdType.MESH)

    for load in loads:
        load.start()
    sends = []
    at = 0
    for z in range(planes):
        for side in range(2):
            loads[at].wait()
            packed = lax.dot_general(
                table_ref[side], edge_y[side, z], (((1,), (1,)), ((), ())),
                preferred_element_type=jnp.float32)
            out_y[side, z] = packed.astype(out_y.dtype)
            if not sends:
                pl.semaphore_wait(barrier, 4)
            sends.append(pltpu.make_async_remote_copy(
                out_y.at[side, z], halo_y_ref.at[side, z], send_sem.at[0, side, z],
                recv_sem.at[0, side, z], device_id=targets[0][side],
                device_id_type=pl.DeviceIdType.MESH))
            sends[-1].start()
            loads[at + 1].wait()
            cut = (LANES - depth) if side == 0 else 0
            packed = mix(table_ref[side][:, cut : cut + depth], edge_x[side, z])
            out_x[side, z] = packed.astype(out_x.dtype)
            sends.append(pltpu.make_async_remote_copy(
                out_x.at[side, z], halo_x_ref.at[side, z], send_sem.at[1, side, z],
                recv_sem.at[1, side, z], device_id=targets[1][side],
                device_id_type=pl.DeviceIdType.MESH))
            sends[-1].start()
            at += 2
    for send in sends:
        send.wait()


def exchange(velocity):
    planes, rows, cols = velocity.shape
    depth = LANES // 2
    dtype = velocity.dtype
    shape_y, shape_x = ((2, planes, PACK, rows), (2, planes, PACK, cols))
    return pl.pallas_call(
        exchange_kernel,
        in_specs=[pl.BlockSpec(memory_space=pl.ANY), pl.BlockSpec(memory_space=pltpu.VMEM)],
        out_specs=[pl.BlockSpec(memory_space=pl.ANY)] * 2,
        out_shape=[jax.ShapeDtypeStruct(shape_y, dtype), jax.ShapeDtypeStruct(shape_x, dtype)],
        scratch_shapes=[
            pltpu.VMEM((2, planes, rows, LANES), dtype),
            pltpu.VMEM((2, planes, depth, cols), dtype),
            pltpu.VMEM(shape_y, dtype),
            pltpu.VMEM(shape_x, dtype),
            pltpu.SemaphoreType.DMA((2, 2, planes)),
            pltpu.SemaphoreType.DMA((2, 2, planes)),
            pltpu.SemaphoreType.DMA((2, 2, planes)),
        ],
        compiler_params=pltpu.CompilerParams(
            collective_id=0, has_side_effects=True, vmem_limit_bytes=48 * 2**20),
    )(velocity, pack_tables())


def main_kernel(
    x_ref, prev_ref, next_ref, before_x_ref, after_x_ref, before_y_ref, after_y_ref,
    tx_ref, ty_ref, th_ref, dx_ref, dy_ref,
):
    rows, cols = x_ref.shape
    step, steps = (pl.program_id(1), pl.num_programs(1))
    empty = jnp.zeros((HALO - PACK, cols), x_ref.dtype)
    for top in range(0, rows, OUT_ROWS):
        low, high = top - HALO, top - HALO + WINDOW
        parts = []
        if low < 0:
            outside = jnp.concatenate([empty, before_x_ref[...]], axis=0)
            parts.append(jnp.where(step == 0, outside, prev_ref[...]))
        parts.append(x_ref[max(low, 0) : min(high, rows), :])
        if high > rows:
            outside = jnp.concatenate([after_x_ref[...], empty], axis=0)
            parts.append(jnp.where(step == steps - 1, outside, next_ref[...]))
        window = jnp.concatenate(parts, axis=0) if len(parts) > 1 else parts[0]
        result = mix(tx_ref[...], window) * SCALE
        dx_ref[top : top + OUT_ROWS, :] = result.astype(dx_ref.dtype)
    for left in range(0, cols, 2 * LANES):
        right = min(left + 2 * LANES, cols)
        low, high = max(left - LANES, 0), min(right + LANES, cols)
        start = low - (left - LANES)
        table = ty_ref[start : start + high - low, : right - left]
        result = mix(x_ref[:, low:high], table)
        blocks = [result[:, k : k + LANES] for k in range(0, right - left, LANES)]
        if left == 0:
            blocks[0] = blocks[0] + mix_first(before_y_ref[...], th_ref[0])
        if right == cols:
            blocks[-1] = blocks[-1] + mix_first(after_y_ref[...], th_ref[1])
        for k, block in enumerate(blocks):
            dy_ref[:, left + k * LANES : left + (k + 1) * LANES] = (block * SCALE).astype(dy_ref.dtype)


def mix_first(a, b):
    return lax.dot_general(a, b, (((0,), (0,)), ((), ())), preferred_element_type=jnp.float32)


def pick_rows(rows, limit):
    best = OUT_ROWS
    for n in range(OUT_ROWS, limit + 1, OUT_ROWS):
        if rows % n == 0:
            best = n
    return best


def shards(velocity):
    planes, rows, cols = velocity.shape
    halo_y, halo_x = exchange(velocity)
    tile = pick_rows(rows, 1536)
    per = tile // HALO
    strips = rows // HALO
    tx = weight_table(np.arange(OUT_ROWS) + HALO, np.arange(WINDOW))
    ty = weight_table(np.arange(2 * LANES) + LANES, np.arange(4 * LANES)).T
    here = np.arange(LANES)
    th = jnp.stack([
        weight_table(here, np.arange(-PACK, 0)).T,
        weight_table(here, np.arange(LANES, LANES + PACK)).T,
    ])
    shape = jax.ShapeDtypeStruct(velocity.shape, velocity.dtype)
    full = pl.BlockSpec((None, tile, cols), lambda z, i: (z, i, 0))
    size = planes * rows * cols

    def ends_x(side):
        return pl.BlockSpec((None, None, PACK, cols), lambda z, i: (side, z, 0, 0))

    def ends_y(side):
        return pl.BlockSpec((None, None, PACK, tile), lambda z, i: (side, z, 0, i))

    return pl.pallas_call(
        main_kernel,
        grid=(planes, rows // tile),
        in_specs=[
            full,
            pl.BlockSpec((None, HALO, cols), lambda z, i: (z, jnp.maximum(i * per - 1, 0), 0)),
            pl.BlockSpec((None, HALO, cols), lambda z, i: (z, jnp.minimum((i + 1) * per, strips - 1), 0)),
            ends_x(0), ends_x(1), ends_y(0), ends_y(1),
            pl.BlockSpec(tx.shape, lambda z, i: (0, 0)),
            pl.BlockSpec(ty.shape, lambda z, i: (0, 0)),
            pl.BlockSpec(th.shape, lambda z, i: (0, 0, 0)),
        ],
        out_specs=[full, full],
        out_shape=[shape, shape],
        cost_estimate=pl.CostEstimate(flops=size * 2 * 1024, bytes_accessed=size * 6, transcendentals=0),
        compiler_params=pltpu.CompilerParams(vmem_limit_bytes=48 * 2**20),
    )(velocity, velocity, velocity, halo_x, halo_x, halo_y, halo_y, tx, ty, th)


def solution(mesh):
    placed = P(None, "narrow", "wide")
    return jax.shard_map(
        shards, mesh=mesh, in_specs=(placed,), out_specs=(placed, placed), check_vma=False
    )
```
